512 devices in a mesh: seq: 64 (over y_hi, z, core), head: 8 (over x, y_lo).
Axes of the slice: x: 4, y: 4 (y_hi: 2, y_lo: 2; y = y_hi * 2 + y_lo), z: 16, core: 2. Of those that a mesh axis runs over, the one named last changes fastest.
Arguments:
- latent: bfloat16 [8192, 576], P('seq'), may hold values from -7 to 7
- queries: bfloat16 [8192, 8, 576], P('seq', 'head'), may hold values from -66 to 66
- grad_out: bfloat16 [8192, 8, 512], P('seq', 'head'), may hold values from -6 to 6
- doc_lengths: int32 [8], replicated, may hold values from 1 to 5120, 8192 in all
Outputs:
- grad_queries: bfloat16 [8192, 8, 576], P('seq', 'head')
- grad_latent: bfloat16 [8192, 576], P(('seq', 'head'))
The draws below stay inside these ranges and needn't reach their ends.
Inputs may be any that keep to these rules, and one draw needn't show every extreme that they name: `doc_lengths`: the lengths sum to 8192; the longest is exactly 5120.
All inputs are finite; a program needn't handle non-finite values.
Results may differ from the reference program's by a relative error of at most 0.0085.
Values may be sent and summed in bfloat16 or wider, within the bound.
A program may use at most 64 MiB of HBM per device.

```python
import math
import jax
import jax.numpy as jnp
import numpy as np
from jax import lax

KV_RANK = 512
LATENT = 576
HEADS = 8
ROWS = 128
TOKENS = 8192
DOCS = 8
MOST = 5120


def base_field(key):
    return jax.random.truncated_normal(key, -6.0, 6.0, (TOKENS, LATENT), jnp.float32)


def drawn_rows(key):
    chosen = jax.random.randint(jax.random.fold_in(key, 11), (TOKENS,), 0, 32)
    return (chosen == 0) & (jnp.arange(TOKENS) >= 1)


def draw_latent(key, part):
    field = base_field(key)
    aligned = drawn_rows(key)
    key = jax.random.fold_in(key, 3)
    spread = 0.01 * LATENT ** 0.5
    jitter = spread * jax.random.truncated_normal(key, -4.0, 4.0, (TOKENS, LATENT), jnp.float32)
    following = jnp.concatenate([field[1:], field[-1:]], 0)
    before_aligned = jnp.concatenate([aligned[1:], jnp.zeros((1,), bool)], 0)
    return jnp.where(before_aligned[:, None], following + jitter, field).astype(jnp.bfloat16)


def lifted_queries(key, field, aligned, top_score):
    independent = jax.random.truncated_normal(key, -6.0, 6.0, (TOKENS, HEADS, LATENT), jnp.float32)
    target = jax.random.uniform(jax.random.fold_in(key, 1), (HEADS,), jnp.float32, 220.0, top_score)
    strength = target / (LATENT * 0.07216878364870322)
    lifted = strength[None, :, None] * field[:, None, :]
    return jnp.where(aligned[:, None, None], lifted, independent).astype(jnp.bfloat16)


def draw_queries(key, part):
    field = base_field(key)
    aligned = drawn_rows(key)
    key = jax.random.fold_in(key, 5)
    return lifted_queries(key, field, aligned, 320.0)


def block_levels(rng, shape, pieces, least, top_value):
    gain = 1.0
    for axis_at, shards_of in pieces:
        draws = jax.random.uniform(jax.random.fold_in(jax.random.fold_in(rng, 6), axis_at), (shards_of,), jnp.float32, least / len(pieces), top_value / len(pieces))
        gain = gain * jnp.repeat(jnp.exp(draws), shape[axis_at] // shards_of).reshape((-1,) + (1,) * (len(shape) - 1 - axis_at))
    return gain


def length_profile(amount, total, reach, slope):
    portions = [(1 << 20) // math.isqrt(grade ** slope) + 1 for grade in range(2, amount + 1)]
    rest, counts = total - reach - (amount - 1), [1] * (amount - 1)
    while rest > 0:
        candidates = [i for i in range(amount - 1) if counts[i] < reach]
        pool, remaining = sum([portions[i] for i in candidates]), rest
        for i in candidates:
            extra = min(reach - counts[i], max(1, remaining * portions[i] // pool), rest)
            counts[i] = counts[i] + extra
            rest = rest - extra
    return np.array([reach] + counts)


def ragged(rng, count, total, limit, slope):
    if count == 2:
        one = jax.random.randint(rng, (), max(1, total - limit), min(limit, total - 1) + 1)
        return jnp.stack([one, total - one])
    tallies = jnp.asarray(length_profile(count, total, limit, slope), jnp.int32)
    twos = (count - 1) // 2
    giver, receiver = tallies[1:1 + 2 * twos:2], tallies[2:2 + 2 * twos:2]
    room = jnp.minimum(giver - 1, limit - receiver)
    shifted = jax.random.randint(jax.random.fold_in(rng, 1), (twos,), 0, 1 << 20) % (room + 1)
    tallies = tallies.at[1:1 + 2 * twos:2].set(giver - shifted).at[2:2 + 2 * twos:2].set(receiver + shifted)
    return tallies[jax.random.permutation(jax.random.fold_in(rng, 2), count)]


def normal_values(rng, dims, width, most, shards=(), kind=jnp.bfloat16):
    factor_of = block_levels(rng, dims, shards, -0.22, 0.18) if shards else 1.0
    entries = jax.random.normal(rng, dims, jnp.float32) * width * factor_of
    return jnp.minimum(jnp.maximum(entries, -most), most).astype(kind)


def setup_inputs(seed: int = 0) -> dict:
    key_list = jax.random.split(jax.random.key(seed), 5)
    return {
        "latent": draw_latent(jax.random.fold_in(key_list[4], 71), 0),
        "queries": draw_queries(jax.random.fold_in(key_list[4], 71), 0),
        "grad_out": normal_values(key_list[2], (TOKENS, HEADS, KV_RANK), 1.0, 6.0, ((0, 64), (1, 8))),
        "doc_lengths": ragged(key_list[3], DOCS, TOKENS, MOST, 2).astype(jnp.int32),
    }


softmax_scale = 0.07216878364870322
far_below = -1.0e30


def document_firsts(doc_lengths, positions):
    lengths = doc_lengths.astype(jnp.int32)
    doc_ends = jnp.cumsum(lengths).astype(jnp.int32)
    doc_firsts = (doc_ends - lengths).astype(jnp.int32)
    inside = doc_firsts[None, :] <= positions[:, None]
    return jnp.max(jnp.where(inside, doc_firsts[None, :], 0), axis=1).astype(jnp.int32)


def reference(latent, queries, grad_out, doc_lengths):
    positions = jnp.arange(TOKENS, dtype=jnp.int32)
    doc_start = document_firsts(doc_lengths, positions)
    key_rows = latent.astype(jnp.float32)
    value_rows = latent[:, :KV_RANK].astype(jnp.float32)
    block_rows = ROWS
    block_total = TOKENS // block_rows

    def one_block(running, block_index):
        first = (block_index * block_rows).astype(jnp.int32)
        query_block = lax.dynamic_slice_in_dim(queries, first, block_rows, 0).astype(jnp.float32)
        grad_block = lax.dynamic_slice_in_dim(grad_out, first, block_rows, 0).astype(jnp.float32)
        start_block = lax.dynamic_slice_in_dim(doc_start, first, block_rows, 0)
        query_places = first + jnp.arange(block_rows, dtype=jnp.int32)
        allowed = (positions[None, :] >= start_block[:, None]) & (positions[None, :] <= query_places[:, None])
        allowed = allowed[:, None, :]
        scores = jnp.einsum("qhd,kd->qhk", query_block, key_rows) * softmax_scale
        largest = jnp.max(jnp.where(allowed, scores, far_below), axis=2)
        weights = jnp.where(allowed, jnp.exp(scores - largest[..., None]), 0.0)
        probabilities = weights / jnp.sum(weights, axis=2)[..., None]
        prob_grad = jnp.einsum("qhv,kv->qhk", grad_block, value_rows)
        centred = jnp.sum(probabilities * prob_grad, axis=2)
        score_grad = (probabilities * (prob_grad - centred[..., None]) * softmax_scale).astype(jnp.bfloat16)
        score_grad = lax.optimization_barrier(score_grad).astype(jnp.float32)
        prob_half = lax.optimization_barrier(probabilities.astype(jnp.bfloat16)).astype(jnp.float32)
        grad_block_q = jnp.einsum("qhk,kd->qhd", score_grad, key_rows).astype(jnp.bfloat16)
        latent_part = jnp.einsum("qhk,qhd->kd", score_grad, query_block)
        value_part = jnp.einsum("qhk,qhv->kv", prob_half, grad_block)
        latent_part = latent_part + jnp.pad(value_part, ((0, 0), (0, LATENT - KV_RANK)))
        return running + latent_part, grad_block_q

    total, grad_blocks = lax.scan(one_block, jnp.zeros((TOKENS, LATENT), jnp.float32), jnp.arange(block_total, dtype=jnp.int32))
    grad_queries = grad_blocks.reshape(TOKENS, HEADS, LATENT)
    return grad_queries, total.astype(jnp.bfloat16)
```

```python
import jax
import jax.numpy as jnp
from jax import lax
from jax.experimental import pallas as pl
from jax.experimental.pallas import tpu as pltpu
from jax.sharding import PartitionSpec as P

MESH = pl.DeviceIdType.MESH
F32, BF16 = jnp.float32, jnp.bfloat16
SCALE = 0.07216878364870322
FAR_BELOW = -1e30
NX, NZ = 4, 16
PIECE = 16
TILE = 256
NT = (((1,), (1,)), ((), ()))
NN = (((1,), (0,)), ((), ()))


def dot(a, b, dims=NN):
    return lax.dot_general(a, b, dims, preferred_element_type=F32)


def kernel(
    lat_ref, q_ref, do_ref, len_ref, dq_out, dk_out,
    krows, kbuf, ktr, kpos, qbuf, obuf, sc, dp, sg, pr,
    stat, comb, dk, ksend, krecv, rs_send, rs_recv, yh_send, yh_recv,
    dq_send, dq_recv, dq_own,
    gq_s, gq_r, go_s, go_r, kz_s, kz_r, kc_s, kc_r, st_s, st_r, dc_s, dc_r, rs_s, rs_r, dq_s, dq_r, misc_s, misc_r,
):
    seq, head = lax.axis_index("seq"), lax.axis_index("head")
    yh, z, c = seq // (2 * NZ), (seq // 2) % NZ, seq % 2
    x, yl = head // 2, head % 2

    def at(dx=0, dyl=0, dz=0, dc=0, dyh=0):
        seq_to = ((yh + dyh) % 2) * (2 * NZ) + ((z + dz + NZ) % NZ) * 2 + (c + dc) % 2
        return seq_to, ((x + dx) % NX) * 2 + (yl + dyl) % 2

    def send(src, dst, ssem, rsem, to):
        copy = pltpu.make_async_remote_copy(src, dst, ssem, rsem, device_id=to, device_id_type=MESH)
        copy.start()
        return copy

    me = at()
    pending = []

    peers = [at(dx=j // 2, dyl=j % 2) for j in range(1, 8)]
    peers += [at(dz=d) for d in (1, -1, 2, -2)]
    peers += [at(dc=1), at(dyh=1, dyl=1), at(dyh=1)]
    barrier = pltpu.get_barrier_semaphore()
    for peer in peers:
        pl.semaphore_signal(barrier, inc=1, device_id=peer, device_id_type=MESH)
    krows[...] = lat_ref[...].T
    pl.semaphore_wait(barrier, len(peers))

    def gather(n, src_slot, slot, to):
        if src_slot is None:
            q_src, o_src = q_ref, do_ref
        else:
            q_src, o_src = qbuf.at[src_slot], obuf.at[pl.ds(src_slot * 128, 128)]
        pending.append(send(q_src, qbuf.at[slot], gq_s.at[n], gq_r.at[slot], to))
        pending.append(send(o_src, obuf.at[pl.ds(slot * 128, 128)], go_s.at[n], go_r.at[slot], to))

    def arrived(slot):
        pltpu.make_async_remote_copy(q_ref, qbuf.at[slot], gq_s.at[0], gq_r.at[slot], device_id=me, device_id_type=MESH).wait_recv()
        pltpu.make_async_remote_copy(do_ref, obuf.at[pl.ds(slot * 128, 128)], go_s.at[0], go_r.at[slot], device_id=me, device_id_type=MESH).wait_recv()

    def chunk(o, core=0):
        return kbuf.at[pl.ds(core * 512 + (o % NZ) * 32, 32)]

    def krelay(o, delta):
        to = o - delta
        pending.append(send(chunk(o), chunk(to), kz_s.at[to % NZ], kz_r.at[to % NZ], at(dz=delta)))

    def kshare(o):
        pending.append(send(chunk(o), chunk(o, 1), kc_s.at[o % NZ], kc_r.at[o % NZ], at(dc=1)))

    def karrived(o):
        pltpu.make_async_remote_copy(chunk(o), chunk(o), kz_s.at[o % NZ], kz_r.at[o % NZ], device_id=me, device_id_type=MESH).wait_recv()

    adj = send(
        krows.at[pl.ds(pl.multiple_of((x * 2 + (1 - yl)) * PIECE, PIECE), PIECE)],
        kbuf.at[pl.ds(PIECE, PIECE)], misc_s.at[0], misc_r.at[0], at(dyh=1, dyl=1))
    gather(0, None, 1, at(dyl=1))
    gather(1, None, 6, at(dx=1))
    gather(2, None, 2, at(dx=-1 + NX))
    qbuf[0] = q_ref[...]
    obuf[pl.ds(0, 128)] = do_ref[...]
    kbuf[pl.ds(0, PIECE)] = krows[pl.ds(pl.multiple_of(head * PIECE, PIECE), PIECE)]

    adj.wait_recv()
    for delta in (-2, 2, -1, 1):
        krelay(0, delta)
    kshare(0)

    row = lax.broadcasted_iota(jnp.int32, kpos.shape, 0)
    r_c, r_z, r_y = row // 512, (row // 32) % NZ, (row // PIECE) % 2
    k_c, k_z, k_y = (c + r_c) % 2, (z + r_z) % NZ, (yh + r_y) % 2
    kpos[...] = (k_y * (2 * NZ) + k_z * 2 + k_c) * 128 + head * PIECE + row % PIECE
    qpos = seq * 128 + lax.broadcasted_iota(jnp.int32, (1, 128), 1)
    first = jnp.zeros((1, 128), jnp.int32)
    start = jnp.int32(0)
    for d in range(8):
        first = jnp.where(qpos >= start, start, first)
        start = start + len_ref[d]
    qpos2 = jnp.concatenate([qpos, qpos], axis=1)
    first2 = jnp.concatenate([first, first], axis=1)

    for o in (2, -2):
        karrived(o)
        krelay(o, -2 if o > 0 else 2)
        krelay(o, -1 if o > 0 else 1)
        kshare(o)
    arrived(1)
    gather(3, 1, 7, at(dx=1))
    gather(4, 1, 3, at(dx=-1 + NX))
    arrived(6)
    gather(5, 6, 4, at(dx=1))
    for o in (4, -4, 6, -6):
        karrived(o)
        if o != -6:
            krelay(o, -2 if o > 0 else 2)
        krelay(o, -1 if o > 0 else 1)
        kshare(o)
    for o in (1, -1, 3, -3, 5, -5, 7, -7, 8):
        karrived(o)
        kshare(o)
    arrived(3)
    gather(6, 3, 5, at(dx=-1 + NX))
    for o in range(NZ):
        pltpu.make_async_remote_copy(chunk(o), chunk(o, 1), kc_s.at[o], kc_r.at[o], device_id=me, device_id_type=MESH).wait_recv()

    def tile_rows(i):
        return pl.ds(pl.multiple_of(i * TILE, TILE), TILE)

    def absolute(slot):
        return ((x + slot // 2) % NX) * 2 + (yl + slot % 2) % 2

    def scores(t):
        qt = jnp.concatenate([qbuf[2 * t], qbuf[2 * t + 1]], axis=1)
        grads = obuf[pl.ds(t * TILE, TILE)]

        def first_pass(i, most):
            rows = tile_rows(i)
            keys = kbuf[rows]
            kp = jnp.concatenate([kpos[rows], kpos[rows]], axis=1)
            s = jnp.where((kp >= first2) & (kp <= qpos2), dot(keys, qt) * SCALE, FAR_BELOW)
            sc[t, rows] = s
            dp[t, rows] = dot(keys[:, :512], grads, NT)
            return jnp.maximum(most, jnp.max(s, axis=0, keepdims=True))

        most = lax.fori_loop(0, 4, first_pass, jnp.full((1, TILE), FAR_BELOW, F32))

        def second_pass(i, sums):
            rows = tile_rows(i)
            e = jnp.exp(sc[t, rows] - most)
            sc[t, rows] = e
            return sums[0] + jnp.sum(e, axis=0, keepdims=True), sums[1] + jnp.sum(e * dp[t, rows], axis=0, keepdims=True)

        zero = jnp.zeros((1, TILE), F32)
        total, weighted = lax.fori_loop(0, 4, second_pass, (zero, zero))
        for n, value in enumerate((most, total, weighted)):
            for half in range(2):
                stat[0, pl.ds(n * 8 + absolute(2 * t + half), 1), :] = value[:, half * 128:(half + 1) * 128]

    ktr[...] = kbuf[...].T
    scores(0)
    arrived(2)
    scores(1)
    arrived(7)
    scores(3)
    arrived(4)
    arrived(5)
    scores(2)

    for j in range(1, 8):
        back = ((-(j // 2)) % NX) * 2 + j % 2
        pending.append(send(stat.at[0], stat.at[back], st_s.at[j], st_r.at[back], at(dx=j // 2, dyl=j % 2)))
    for j in range(1, 8):
        pltpu.make_async_remote_copy(stat.at[0], stat.at[j], st_s.at[j], st_r.at[j], device_id=me, device_id_type=MESH).wait_recv()
    most = stat[0, 0:8]
    for j in range(1, 8):
        most = jnp.maximum(most, stat[j, 0:8])
    total, weighted = jnp.zeros((8, 128), F32), jnp.zeros((8, 128), F32)
    for j in range(8):
        factor = jnp.exp(stat[j, 0:8] - most)
        total += stat[j, 8:16] * factor
        weighted += stat[j, 16:24] * factor
    comb[0:8] = jnp.exp(stat[0, 0:8] - most) / total
    comb[8:16] = weighted / total

    for t in range(4):
        def row_of(n):
            return jnp.concatenate([comb[pl.ds(n * 8 + absolute(2 * t + half), 1), :] for half in range(2)], axis=1)

        gain, centre = row_of(0), row_of(1)

        def grads_of(i, carry):
            rows = tile_rows(i)
            p = sc[t, rows] * gain
            sg[rows, t * TILE:(t + 1) * TILE] = (p * (dp[t, rows] - centre) * SCALE).astype(BF16)
            pr[rows, t * TILE:(t + 1) * TILE] = p.astype(BF16)
            return carry

        lax.fori_loop(0, 4, grads_of, 0)

    def dk_tile(rows):
        whole = jnp.zeros((TILE, 576), F32)
        value = jnp.zeros((TILE, 512), F32)
        for t in range(4):
            cols = slice(t * TILE, (t + 1) * TILE)
            qt = jnp.concatenate([qbuf[2 * t], qbuf[2 * t + 1]], axis=1)
            whole += dot(sg[rows, cols], qt, NT)
            value += dot(pr[rows, cols], obuf[pl.ds(t * TILE, TILE)])
        return whole, value

    for half in range(2):
        whole, value = dk_tile(pl.ds(512 + half * TILE, TILE))
        rows = pl.ds(half * TILE, TILE)
        ksend[rows, :512] = (whole[:, :512] + value).astype(BF16)
        ksend[rows, 512:] = whole[:, 512:].astype(BF16)
        pending.append(send(ksend.at[rows], krecv.at[rows], dc_s.at[half], dc_r.at[half], at(dc=1)))
    for half in range(2):
        rows = pl.ds(half * TILE, TILE)
        whole, value = dk_tile(rows)
        dk[rows, :512] = whole[:, :512] + value
        dk[rows, 512:] = whole[:, 512:]
    for half in range(2):
        rows = pl.ds(half * TILE, TILE)
        pltpu.make_async_remote_copy(ksend.at[rows], krecv.at[rows], dc_s.at[half], dc_r.at[half], device_id=me, device_id_type=MESH).wait_recv()

    def rs_wait(o):
        i = o % NZ
        pltpu.make_async_remote_copy(rs_send.at[i], rs_recv.at[i], rs_s.at[i], rs_r.at[i], device_id=me, device_id_type=MESH).wait_recv()
        return rs_recv[i].astype(F32)

    def part(o, sources):
        rows = pl.ds((o % NZ) * 32, 32)
        acc = dk[rows] + krecv[rows].astype(F32)
        for source in sources:
            acc += rs_wait(source)
        return acc

    def rs_pass(o, delta, sources):
        i = o % NZ
        rs_send[i] = part(o, sources).astype(BF16)
        pending.append(send(rs_send.at[i], rs_recv.at[i], rs_s.at[i], rs_r.at[i], at(dz=delta)))

    def dq_pair(t):
        both = dot(ktr[...], sg[:, t * TILE:(t + 1) * TILE])
        for half in range(2):
            j = 2 * t + half
            value = both[:, half * 128:(half + 1) * 128]
            if j == 0:
                dq_own[...] = value
                continue
            dq_send[j] = value.astype(BF16)
            back = ((-(j // 2)) % NX) * 2 + j % 2
            pending.append(send(dq_send.at[j], dq_recv.at[back], dq_s.at[j], dq_r.at[back], at(dx=j // 2, dyl=j % 2)))

    rs_pass(8, 2, ())
    for o in (7, -7, 5, -5, 3, -3, 1, -1):
        rs_pass(o, 1 if o > 0 else -1, ())
    dq_pair(2)
    rs_pass(6, 2, (7, 8))
    rs_pass(-6, -2, (-7,))
    dq_pair(1)
    rs_pass(4, 2, (5, 6))
    rs_pass(-4, -2, (-5, -6))
    dq_pair(3)
    rs_pass(2, 2, (3, 4))
    rs_pass(-2, -2, (-3, -4))
    dq_pair(0)
    mine = part(0, (1, -1, 2, -2))
    yh_send[...] = mine[PIECE:].astype(BF16)
    last = send(yh_send, yh_recv, misc_s.at[1], misc_r.at[1], at(dyh=1))
    dq = dq_own[...]
    for j in range(1, 8):
        pltpu.make_async_remote_copy(dq_send.at[j], dq_recv.at[j], dq_s.at[j], dq_r.at[j], device_id=me, device_id_type=MESH).wait_recv()
        dq += dq_recv[j].astype(F32)
    dq_out[...] = dq.astype(BF16)
    last.wait_recv()
    dk_out[...] = (mine[:PIECE] + yh_recv[...].astype(F32)).astype(BF16)

    adj.wait_send()
    last.wait_send()
    for copy in pending:
        copy.wait_send()


def local(latent, queries, grad_out, doc_lengths):
    vmem = pl.BlockSpec(memory_space=pltpu.VMEM)
    sem = pltpu.SemaphoreType.DMA
    dq, dk = pl.pallas_call(
        kernel,
        out_shape=(jax.ShapeDtypeStruct((576, 128), BF16), jax.ShapeDtypeStruct((PIECE, 576), BF16)),
        in_specs=[vmem, vmem, vmem, pl.BlockSpec(memory_space=pltpu.SMEM)],
        out_specs=(vmem, vmem),
        scratch_shapes=[
            pltpu.VMEM((128, 576), BF16),
            pltpu.VMEM((1024, 576), BF16),
            pltpu.VMEM((576, 1024), BF16),
            pltpu.VMEM((1024, 128), jnp.int32),
            pltpu.VMEM((8, 576, 128), BF16),
            pltpu.VMEM((1024, 512), BF16),
            pltpu.VMEM((4, 1024, TILE), F32),
            pltpu.VMEM((4, 1024, TILE), F32),
            pltpu.VMEM((1024, 1024), BF16),
            pltpu.VMEM((1024, 1024), BF16),
            pltpu.VMEM((8, 24, 128), F32),
            pltpu.VMEM((16, 128), F32),
            pltpu.VMEM((512, 576), F32),
            pltpu.VMEM((512, 576), BF16),
            pltpu.VMEM((512, 576), BF16),
            pltpu.VMEM((NZ, 32, 576), BF16),
            pltpu.VMEM((NZ, 32, 576), BF16),
            pltpu.VMEM((PIECE, 576), BF16),
            pltpu.VMEM((PIECE, 576), BF16),
            pltpu.VMEM((8, 576, 128), BF16),
            pltpu.VMEM((8, 576, 128), BF16),
            pltpu.VMEM((576, 128), F32),
            sem((7,)), sem((8,)), sem((7,)), sem((8,)),
            sem((NZ,)), sem((NZ,)), sem((NZ,)), sem((NZ,)),
            sem((8,)), sem((8,)), sem((2,)), sem((2,)),
            sem((NZ,)), sem((NZ,)), sem((8,)), sem((8,)), sem((2,)), sem((2,)),
        ],
        compiler_params=pltpu.CompilerParams(collective_id=0, has_side_effects=True, vmem_limit_bytes=48 << 20),
        cost_estimate=pl.CostEstimate(flops=6_000_000_000, bytes_accessed=1_000_000, transcendentals=1_100_000),
        name="latent_attention_backward",
    )(latent.T, queries.reshape(128, 576).T, grad_out.reshape(128, 512), doc_lengths)
    return dq.T.reshape(128, 1, 576), dk


def solution(mesh):
    placed = (P("seq", None), P("seq", "head", None), P("seq", "head", None), P())
    return jax.shard_map(
        local,
        mesh=mesh,
        in_specs=placed,
        out_specs=(P("seq", "head", None), P(("seq", "head"), None)),
        check_vma=False,
    )
```

```python
import jax
import jax.numpy as jnp
from jax import lax
from jax.experimental import pallas as pl
from jax.experimental.pallas import tpu as pltpu
from jax.sharding import PartitionSpec as P

MESH = pl.DeviceIdType.MESH
F32, BF16 = jnp.float32, jnp.bfloat16
SCALE = 0.07216878364870322
FAR_BELOW = -1e30
NX, NZ = 4, 16
PIECE = 16
TILE = 256
NT = (((1,), (1,)), ((), ()))
NN = (((1,), (0,)), ((), ()))


def dot(a, b, dims=NN):
    return lax.dot_general(a, b, dims, preferred_element_type=F32)


def tree(step):
    above = {}
    for o in range(1, 9):
        above[o] = (o - 1) // step * step
    for o in range(1, 8):
        above[-o] = -((o - 1) // step * step)
    return above


GATHER, REDUCE = tree(3), tree(3)


def children(above, o):
    return sorted((k for k in above if above[k] == o), key=lambda k: (k not in above.values(), -abs(k), k))


def index(o):
    return (o + 3) % NZ


def kernel(
    lat_ref, q_ref, do_ref, len_ref, dq_out, dk_out,
    lat, krows, kbuf, ktr, kpos, qbuf, obuf, sc, dp, sg, pr,
    stat, comb, dk, ksend, krecv, rs_send, rs_recv, cross_recv,
    dq_send, dq_recv, dq_own,
    gq_s, gq_r, go_s, go_r, kz_s, kz_r, ka_s, ka_r, kc_s, kc_r, st_s, st_r, dc_s, dc_r, rs_s, rs_r, cr_s, cr_r, dq_s, dq_r, here_s,
):
    seq, head = lax.axis_index("seq"), lax.axis_index("head")
    yh, z, c = seq // (2 * NZ), (seq // 2) % NZ, seq % 2
    x, yl = head // 2, head % 2

    def at(dx=0, dyl=0, dz=0, dc=0, dyh=0):
        seq_to = ((yh + dyh) % 2) * (2 * NZ) + ((z + dz + NZ) % NZ) * 2 + (c + dc) % 2
        return seq_to, ((x + dx + NX) % NX) * 2 + (yl + dyl) % 2

    me = at()
    pending = []
    near = children(GATHER, 0)

    def remote(src, dst, ssem, rsem, to):
        return pltpu.make_async_remote_copy(src, dst, ssem, rsem, device_id=to, device_id_type=MESH)

    def send(*args):
        copy = remote(*args)
        copy.start()
        pending.append(copy)

    own = [
        pltpu.make_async_copy(lat_ref, lat, here_s.at[0]),
        pltpu.make_async_copy(q_ref, qbuf.at[0], here_s.at[1]),
        pltpu.make_async_copy(do_ref, obuf.at[pl.ds(0, 128)], here_s.at[2]),
    ]
    for copy in own:
        copy.start()
    peers = [at(dx=j // 2, dyl=j % 2) for j in range(1, 8)]
    peers += [at(dz=o) for o in near]
    peers += [at(dyh=1, dyl=1, dz=o) for o in [0] + near]
    peers += [at(dyh=1, dz=o) for o in [0] + near]
    peers += [at(dc=1)]
    barrier = pltpu.get_barrier_semaphore()
    for peer in peers:
        pl.semaphore_signal(barrier, inc=1, device_id=peer, device_id_type=MESH)
    own[0].wait()
    krows[...] = lat[...].T
    own[1].wait()
    own[2].wait()
    pl.semaphore_wait(barrier, len(peers))

    def grad_rows(slot):
        return obuf.at[pl.ds(slot * 128, 128)]

    def gather_q(n, src, slot, to):
        send(qbuf.at[src], qbuf.at[slot], gq_s.at[n], gq_r.at[slot], to)

    def gather_o(n, src, slot, to):
        send(grad_rows(src), grad_rows(slot), go_s.at[n], go_r.at[slot], to)

    def gather(n, src, slot, to):
        gather_q(n, src, slot, to)
        gather_o(n, src, slot, to)

    def arrived_q(slot):
        remote(qbuf.at[0], qbuf.at[slot], gq_s.at[0], gq_r.at[slot], me).wait_recv()

    def arrived_o(slot):
        remote(grad_rows(0), grad_rows(slot), go_s.at[0], go_r.at[slot], me).wait_recv()

    def chunk(o, core=0):
        return kbuf.at[pl.ds(core * 512 + index(o) * 32, 32)]

    def piece(o, plane):
        return kbuf.at[pl.ds(index(o) * 32 + plane * PIECE, PIECE)]

    own_piece = krows.at[pl.ds(pl.multiple_of(head * PIECE, PIECE), PIECE)]
    their_piece = krows.at[pl.ds(pl.multiple_of((x * 2 + (1 - yl)) * PIECE, PIECE), PIECE)]

    def first_spread(o):
        i = index(o)
        if o != 0:
            send(own_piece, piece(o, 0), kz_s.at[i], kz_r.at[i], at(dz=-o))
        send(their_piece, piece(o, 1), ka_s.at[i], ka_r.at[i], at(dyh=1, dyl=1, dz=-o))

    def share(o):
        i = index(o)
        send(chunk(o), chunk(o, 1), kc_s.at[i], kc_r.at[i], at(dc=1))

    def spread(o):
        for to in children(GATHER, o):
            n = index(to)
            send(chunk(o), chunk(to), kz_s.at[n], kz_r.at[n], at(dz=o - to))
        share(o)

    def karrived(o):
        i = index(o)
        if o in near:
            remote(own_piece, piece(o, 0), kz_s.at[i], kz_r.at[i], me).wait_recv()
        elif o != 0:
            remote(chunk(o), chunk(o), kz_s.at[i], kz_r.at[i], me).wait_recv()
        if o in near or o == 0:
            remote(their_piece, piece(o, 1), ka_s.at[i], ka_r.at[i], me).wait_recv()

    for o in near[:2]:
        first_spread(o)
    gather(0, 0, 6, at(dx=1))
    gather(1, 0, 2, at(dx=-1))
    gather(2, 0, 1, at(dyl=1))
    for o in [0] + near[2:]:
        first_spread(o)
    kbuf[pl.ds(index(0) * 32, PIECE)] = krows[pl.ds(pl.multiple_of(head * PIECE, PIECE), PIECE)]

    row = lax.broadcasted_iota(jnp.int32, kpos.shape, 0)
    r_c, r_z, r_y = row // 512, (row // 32) % NZ, (row // PIECE) % 2
    k_c, k_z, k_y = (c + r_c) % 2, (z + r_z + NZ - 3) % NZ, (yh + r_y) % 2
    kpos[...] = (k_y * (2 * NZ) + k_z * 2 + k_c) * 128 + head * PIECE + row % PIECE
    qpos = seq * 128 + lax.broadcasted_iota(jnp.int32, (1, 128), 1)
    first = jnp.zeros((1, 128), jnp.int32)
    start = jnp.int32(0)
    for d in range(8):
        first = jnp.where(qpos >= start, start, first)
        start = start + len_ref[d]
    qpos2 = jnp.concatenate([qpos, qpos], axis=1)
    first2 = jnp.concatenate([first, first], axis=1)
    waits = sorted(GATHER, key=lambda o: (abs(o), -o))
    hubs = [o for o in waits if children(GATHER, o)]
    for o in hubs[:2]:
        karrived(o)
        spread(o)
    arrived_q(6)
    gather_q(3, 6, 4, at(dx=1))
    arrived_o(2)
    gather_o(3, 2, 4, at(dx=-1))
    karrived(0)
    share(0)
    arrived_q(1)
    gather_q(4, 1, 7, at(dx=1))
    gather_q(5, 1, 3, at(dx=-1))
    arrived_o(1)
    gather_o(4, 1, 7, at(dx=1))
    gather_o(5, 1, 3, at(dx=-1))
    for o in hubs[2:]:
        karrived(o)
        spread(o)
    arrived_q(4)
    gather_q(6, 4, 5, at(dyl=1))
    arrived_o(4)
    gather_o(6, 4, 5, at(dyl=1))
    for o in waits:
        if o not in hubs:
            karrived(o)
            share(o)
    arrived_o(6)
    arrived_q(2)
    for o in range(NZ):
        i = index(o)
        remote(chunk(o), chunk(o, 1), kc_s.at[i], kc_r.at[i], me).wait_recv()

    def absolute(slot):
        return ((x + slot // 2) % NX) * 2 + (yl + slot % 2) % 2

    def queries_of(t):
        return jnp.concatenate([qbuf[2 * t], qbuf[2 * t + 1]], axis=1)

    def scores(t):
        qt = queries_of(t)
        grads = obuf[pl.ds(t * TILE, TILE)]
        most = jnp.full((1, TILE), FAR_BELOW, F32)
        for i in range(4):
            rows = pl.ds(i * TILE, TILE)
            keys = kbuf[rows]
            kp = jnp.concatenate([kpos[rows], kpos[rows]], axis=1)
            s = jnp.where((kp >= first2) & (kp <= qpos2), dot(keys, qt) * SCALE, FAR_BELOW)
            sc[t, rows] = s
            dp[t, rows] = dot(keys[:, :512], grads, NT)
            most = jnp.maximum(most, jnp.max(s, axis=0, keepdims=True))
        total = weighted = jnp.zeros((1, TILE), F32)
        for i in range(4):
            rows = pl.ds(i * TILE, TILE)
            e = jnp.exp(sc[t, rows] - most)
            sc[t, rows] = e
            total += jnp.sum(e, axis=0, keepdims=True)
            weighted += jnp.sum(e * dp[t, rows], axis=0, keepdims=True)
        for n, value in enumerate((most, total, weighted)):
            for half in range(2):
                stat[0, pl.ds(n * 8 + absolute(2 * t + half), 1), :] = value[:, half * 128:(half + 1) * 128]

    scores(0)
    for t in (1, 3, 2):
        for slot in {1: (3,), 3: (7,), 2: (5,)}[t]:
            arrived_q(slot)
            arrived_o(slot)
        scores(t)

    for j in (4, 5, 3, 7, 1, 2, 6):
        back = ((-(j // 2)) % NX) * 2 + j % 2
        send(stat.at[0], stat.at[back], st_s.at[j], st_r.at[back], at(dx=j // 2, dyl=j % 2))
    ktr[...] = kbuf[...].T
    for j in range(1, 8):
        remote(stat.at[0], stat.at[j], st_s.at[j], st_r.at[j], me).wait_recv()
    most = stat[0, 0:8]
    for j in range(1, 8):
        most = jnp.maximum(most, stat[j, 0:8])
    total, weighted = jnp.zeros((8, 128), F32), jnp.zeros((8, 128), F32)
    for j in range(8):
        factor = jnp.exp(stat[j, 0:8] - most)
        total += stat[j, 8:16] * factor
        weighted += stat[j, 16:24] * factor
    comb[0:8] = jnp.exp(stat[0, 0:8] - most) / total
    comb[8:16] = weighted / total

    def grads_of(i):
        rows = pl.ds(i * TILE, TILE)
        for t in range(4):
            gain, centre = (
                jnp.concatenate([comb[pl.ds(n * 8 + absolute(2 * t + half), 1), :] for half in range(2)], axis=1) for n in range(2))
            p = sc[t, rows] * gain
            sg[rows, t * TILE:(t + 1) * TILE] = (p * (dp[t, rows] - centre) * SCALE).astype(BF16)
            pr[rows, t * TILE:(t + 1) * TILE] = p.astype(BF16)

    def dk_tile(i, out, out_rows):
        rows = pl.ds(i * TILE, TILE)
        value = dot(pr[rows], obuf[...])
        whole = jnp.zeros((TILE, 576), F32)
        for t in range(4):
            whole += dot(sg[rows, t * TILE:(t + 1) * TILE], queries_of(t), NT)
        out[out_rows, :512] = (whole[:, :512] + value).astype(out.dtype)
        out[out_rows, 512:] = whole[:, 512:].astype(out.dtype)

    def dk_other(half):
        rows = pl.ds(half * TILE, TILE)
        dk_tile(2 + half, ksend, rows)
        send(ksend.at[rows], krecv.at[rows], dc_s.at[half], dc_r.at[half], at(dc=1))

    def dk_own(half):
        dk_tile(half, dk, pl.ds(half * TILE, TILE))

    def other_core(half):
        rows = pl.ds(half * TILE, TILE)
        remote(ksend.at[rows], krecv.at[rows], dc_s.at[half], dc_r.at[half], me).wait_recv()

    def part(o):
        rows = pl.ds(index(o) * 32, 32)
        acc = dk[rows] + krecv[rows].astype(F32)
        for source in children(REDUCE, o):
            i = index(source)
            remote(rs_send.at[i], rs_recv.at[i], rs_s.at[i], rs_r.at[i], me).wait_recv()
            acc += rs_recv[i].astype(F32)
        return acc

    def first_half(ref, o):
        return ref.at[index(o), pl.ds(0, PIECE)]

    def rs_pass(o):
        i = index(o)
        rs_send[i] = part(o).astype(BF16)
        if REDUCE[o] != 0:
            send(rs_send.at[i], rs_recv.at[i], rs_s.at[i], rs_r.at[i], at(dz=o - REDUCE[o]))
            return
        cross(o)
        send(first_half(rs_send, o), first_half(rs_recv, o), rs_s.at[i], rs_r.at[i], at(dz=o))

    def cross(o):
        i = index(o)
        send(rs_send.at[i, pl.ds(PIECE, PIECE)], cross_recv.at[i], cr_s.at[i], cr_r.at[i], at(dyh=1, dz=o))

    def dq_pair(t):
        both = dot(ktr[...], sg[:, t * TILE:(t + 1) * TILE])
        for half in range(2):
            j = 2 * t + half
            value = both[:, half * 128:(half + 1) * 128]
            if j == 0:
                dq_own[...] = value
                continue
            dq_send[j] = value.astype(BF16)
            back = ((-(j // 2)) % NX) * 2 + j % 2
            send(dq_send.at[j], dq_recv.at[back], dq_s.at[j], dq_r.at[back], at(dx=j // 2, dyl=j % 2))

    leaves = sorted((o for o in REDUCE if not children(REDUCE, o)), key=lambda o: (-abs(o), -o))
    inner = sorted((o for o in REDUCE if children(REDUCE, o)), key=lambda o: (-abs(o), -o))
    early = [o for o in leaves if index(o) >= 8]
    grads_of(3)
    dk_other(1)
    grads_of(1)
    dk_own(1)
    grads_of(2)
    grads_of(0)
    dq_pair(2)
    other_core(1)
    for o in early:
        rs_pass(o)
    dk_other(0)
    dk_own(0)
    dq_pair(1)
    other_core(0)
    for o in leaves:
        if o not in early:
            rs_pass(o)
    rs_send[index(0), PIECE:] = (dk[pl.ds(index(0) * 32 + PIECE, PIECE)] + krecv[pl.ds(index(0) * 32 + PIECE, PIECE)].astype(F32)).astype(BF16)
    cross(0)
    dq_pair(3)
    for o in inner[:2]:
        rs_pass(o)
    dq_pair(0)
    for o in inner[2:]:
        rs_pass(o)
    dq = dq_own[...]
    for j in (1, 2, 3, 6, 7, 4, 5):
        remote(dq_send.at[j], dq_recv.at[j], dq_s.at[j], dq_r.at[j], me).wait_recv()
        dq += dq_recv[j].astype(F32)
    dq_out[...] = dq.astype(BF16)
    rows = pl.ds(index(0) * 32, PIECE)
    total = dk[rows] + krecv[rows].astype(F32)
    for o in children(REDUCE, 0):
        i = index(o)
        remote(first_half(rs_send, o), first_half(rs_recv, o), rs_s.at[i], rs_r.at[i], me).wait_recv()
        total += rs_recv[i, :PIECE].astype(F32)
    for o in [0] + children(REDUCE, 0):
        i = index(o)
        remote(rs_send.at[i, pl.ds(PIECE, PIECE)], cross_recv.at[i], cr_s.at[i], cr_r.at[i], me).wait_recv()
        total += cross_recv[i].astype(F32)
    dk_out[...] = total.astype(BF16)
    for copy in pending:
        copy.wait_send()


def local(latent, queries, grad_out, doc_lengths):
    vmem = pl.BlockSpec(memory_space=pltpu.VMEM)
    hbm = pl.BlockSpec(memory_space=pltpu.HBM)
    sem = pltpu.SemaphoreType.DMA
    dq, dk = pl.pallas_call(
        kernel,
        out_shape=(jax.ShapeDtypeStruct((576, 128), BF16), jax.ShapeDtypeStruct((PIECE, 576), BF16)),
        in_specs=[hbm, hbm, hbm, pl.BlockSpec(memory_space=pltpu.SMEM)],
        out_specs=(vmem, vmem),
        scratch_shapes=[
            pltpu.VMEM((576, 128), BF16),
            pltpu.VMEM((128, 576), BF16),
            pltpu.VMEM((1024, 576), BF16),
            pltpu.VMEM((576, 1024), BF16),
            pltpu.VMEM((1024, 128), jnp.int32),
            pltpu.VMEM((8, 576, 128), BF16),
            pltpu.VMEM((1024, 512), BF16),
            pltpu.VMEM((4, 1024, TILE), F32),
            pltpu.VMEM((4, 1024, TILE), F32),
            pltpu.VMEM((1024, 1024), BF16),
            pltpu.VMEM((1024, 1024), BF16),
            pltpu.VMEM((8, 24, 128), F32),
            pltpu.VMEM((16, 128), F32),
            pltpu.VMEM((512, 576), F32),
            pltpu.VMEM((512, 576), BF16),
            pltpu.VMEM((512, 576), BF16),
            pltpu.VMEM((NZ, 32, 576), BF16),
            pltpu.VMEM((NZ, 32, 576), BF16),
            pltpu.VMEM((NZ, PIECE, 576), BF16),
            pltpu.VMEM((8, 576, 128), BF16),
            pltpu.VMEM((8, 576, 128), BF16),
            pltpu.VMEM((576, 128), F32),
            sem((7,)), sem((8,)), sem((7,)), sem((8,)),
            sem((NZ,)), sem((NZ,)), sem((NZ,)), sem((NZ,)), sem((NZ,)), sem((NZ,)),
            sem((8,)), sem((8,)), sem((2,)), sem((2,)),
            sem((NZ,)), sem((NZ,)), sem((NZ,)), sem((NZ,)), sem((8,)), sem((8,)), sem((3,)),
        ],
        compiler_params=pltpu.CompilerParams(collective_id=0, has_side_effects=True, vmem_limit_bytes=60 << 20),
        cost_estimate=pl.CostEstimate(flops=6_000_000_000, bytes_accessed=1_000_000, transcendentals=1_100_000),
        name="latent_attention_backward",
    )(latent.T, queries.reshape(128, 576).T, grad_out.reshape(128, 512), doc_lengths)
    return dq.T.reshape(128, 1, 576), dk


def solution(mesh):
    placed = (P("seq", None), P("seq", "head", None), P("seq", "head", None), P())
    return jax.shard_map(
        local,
        mesh=mesh,
        in_specs=placed,
        out_specs=(P("seq", "head", None), P(("seq", "head"), None)),
        check_vma=False,
    )
```

```python
import jax
import jax.numpy as jnp
from jax import lax
from jax.experimental import pallas as pl
from jax.experimental.pallas import tpu as pltpu
from jax.sharding import PartitionSpec as P

MESH = pl.DeviceIdType.MESH
F32, BF16 = jnp.float32, jnp.bfloat16
SCALE = 0.07216878364870322
FAR_BELOW = -1e30
NX, NZ = 4, 16
PIECE = 16
TILE = 256
NT = (((1,), (1,)), ((), ()))
NN = (((1,), (0,)), ((), ()))


def dot(a, b, dims=NN):
    return lax.dot_general(a, b, dims, preferred_element_type=F32)


def tree(step):
    above = {}
    for o in range(1, 9):
        above[o] = (o - 1) // step * step
    for o in range(1, 8):
        above[-o] = -((o - 1) // step * step)
    return above


GATHER, REDUCE = tree(3), tree(2)


def children(above, o):
    return sorted((k for k in above if above[k] == o), key=lambda k: (k not in above.values(), -abs(k), k))


def index(o):
    return (o + 3) % NZ


def kernel(
    lat_ref, q_ref, do_ref, len_ref, dq_out, dk_out,
    lat, krows, kbuf, ktr, kpos, qbuf, obuf, sc, dp, sg, pr,
    stat, comb, dk, ksend, krecv, rs_send, rs_recv, cross_recv,
    dq_send, dq_recv, dq_own,
    gq_s, gq_r, go_s, go_r, kz_s, kz_r, ka_s, ka_r, kc_s, kc_r, st_s, st_r, dc_s, dc_r, rs_s, rs_r, cr_s, cr_r, dq_s, dq_r, here_s,
):
    seq, head = lax.axis_index("seq"), lax.axis_index("head")
    yh, z, c = seq // (2 * NZ), (seq // 2) % NZ, seq % 2
    x, yl = head // 2, head % 2

    def at(dx=0, dyl=0, dz=0, dc=0, dyh=0):
        seq_to = ((yh + dyh) % 2) * (2 * NZ) + ((z + dz + NZ) % NZ) * 2 + (c + dc) % 2
        return seq_to, ((x + dx + NX) % NX) * 2 + (yl + dyl) % 2

    me = at()
    pending = []
    near = children(GATHER, 0)

    def remote(src, dst, ssem, rsem, to):
        return pltpu.make_async_remote_copy(src, dst, ssem, rsem, device_id=to, device_id_type=MESH)

    def send(*args):
        copy = remote(*args)
        copy.start()
        pending.append(copy)

    own = [
        pltpu.make_async_copy(lat_ref, lat, here_s.at[0]),
        pltpu.make_async_copy(q_ref, qbuf.at[0], here_s.at[1]),
        pltpu.make_async_copy(do_ref, obuf.at[pl.ds(0, 128)], here_s.at[2]),
    ]
    for copy in own:
        copy.start()
    peers = [at(dx=j // 2, dyl=j % 2) for j in range(1, 8)]
    peers += [at(dz=o) for o in near]
    peers += [at(dyh=1, dyl=1, dz=o) for o in [0] + near]
    peers += [at(dyh=1, dz=o) for o in [0] + near]
    peers += [at(dc=1)]
    barrier = pltpu.get_barrier_semaphore()
    for peer in peers:
        pl.semaphore_signal(barrier, inc=1, device_id=peer, device_id_type=MESH)
    own[0].wait()
    krows[...] = lat[...].T
    own[1].wait()
    own[2].wait()
    pl.semaphore_wait(barrier, len(peers))

    def grad_rows(slot):
        return obuf.at[pl.ds(slot * 128, 128)]

    def gather_q(n, src, slot, to):
        send(qbuf.at[src], qbuf.at[slot], gq_s.at[n], gq_r.at[slot], to)

    def gather_o(n, src, slot, to):
        send(grad_rows(src), grad_rows(slot), go_s.at[n], go_r.at[slot], to)

    def gather(n, src, slot, to):
        gather_q(n, src, slot, to)
        gather_o(n, src, slot, to)

    def arrived_q(slot):
        remote(qbuf.at[0], qbuf.at[slot], gq_s.at[0], gq_r.at[slot], me).wait_recv()

    def arrived_o(slot):
        remote(grad_rows(0), grad_rows(slot), go_s.at[0], go_r.at[slot], me).wait_recv()

    def chunk(o, core=0):
        return kbuf.at[pl.ds(core * 512 + index(o) * 32, 32)]

    def piece(o, plane):
        return kbuf.at[pl.ds(index(o) * 32 + plane * PIECE, PIECE)]

    own_piece = krows.at[pl.ds(pl.multiple_of(head * PIECE, PIECE), PIECE)]
    their_piece = krows.at[pl.ds(pl.multiple_of((x * 2 + (1 - yl)) * PIECE, PIECE), PIECE)]

    def first_spread(o):
        i = index(o)
        if o != 0:
            send(own_piece, piece(o, 0), kz_s.at[i], kz_r.at[i], at(dz=-o))
        send(their_piece, piece(o, 1), ka_s.at[i], ka_r.at[i], at(dyh=1, dyl=1, dz=-o))

    def share(o):
        i = index(o)
        send(chunk(o), chunk(o, 1), kc_s.at[i], kc_r.at[i], at(dc=1))

    def spread(o):
        for to in children(GATHER, o):
            n = index(to)
            send(chunk(o), chunk(to), kz_s.at[n], kz_r.at[n], at(dz=o - to))
        share(o)

    def karrived(o):
        i = index(o)
        if o in near:
            remote(own_piece, piece(o, 0), kz_s.at[i], kz_r.at[i], me).wait_recv()
        elif o != 0:
            remote(chunk(o), chunk(o), kz_s.at[i], kz_r.at[i], me).wait_recv()
        if o in near or o == 0:
            remote(their_piece, piece(o, 1), ka_s.at[i], ka_r.at[i], me).wait_recv()

    for o in near[:2]:
        first_spread(o)
    gather(0, 0, 6, at(dx=1))
    gather(1, 0, 2, at(dx=-1))
    gather(2, 0, 1, at(dyl=1))
    for o in [0] + near[2:]:
        first_spread(o)
    kbuf[pl.ds(index(0) * 32, PIECE)] = krows[pl.ds(pl.multiple_of(head * PIECE, PIECE), PIECE)]

    row = lax.broadcasted_iota(jnp.int32, kpos.shape, 0)
    r_c, r_z, r_y = row // 512, (row // 32) % NZ, (row // PIECE) % 2
    k_c, k_z, k_y = (c + r_c) % 2, (z + r_z + NZ - 3) % NZ, (yh + r_y) % 2
    kpos[...] = (k_y * (2 * NZ) + k_z * 2 + k_c) * 128 + head * PIECE + row % PIECE
    qpos = seq * 128 + lax.broadcasted_iota(jnp.int32, (1, 128), 1)
    first = jnp.zeros((1, 128), jnp.int32)
    start = jnp.int32(0)
    for d in range(8):
        first = jnp.where(qpos >= start, start, first)
        start = start + len_ref[d]
    qpos2 = jnp.concatenate([qpos, qpos], axis=1)
    first2 = jnp.concatenate([first, first], axis=1)
    waits = sorted(GATHER, key=lambda o: (abs(o), -o))
    hubs = [o for o in waits if children(GATHER, o)]
    for o in hubs[:2]:
        karrived(o)
        spread(o)
    arrived_q(6)
    gather_q(3, 6, 4, at(dx=1))
    arrived_o(2)
    gather_o(3, 2, 4, at(dx=-1))
    karrived(0)
    share(0)
    arrived_q(1)
    gather_q(4, 1, 7, at(dx=1))
    gather_q(5, 1, 3, at(dx=-1))
    arrived_o(1)
    gather_o(4, 1, 7, at(dx=1))
    gather_o(5, 1, 3, at(dx=-1))
    for o in hubs[2:]:
        karrived(o)
        spread(o)
    arrived_q(4)
    gather_q(6, 4, 5, at(dyl=1))
    arrived_o(4)
    gather_o(6, 4, 5, at(dyl=1))
    most, total, weighted = {}, {}, {}

    def absolute(slot):
        return ((x + slot // 2) % NX) * 2 + (yl + slot % 2) % 2

    def queries_of(t):
        return jnp.concatenate([qbuf[2 * t], qbuf[2 * t + 1]], axis=1)

    def scores(t, tiles):
        qt = queries_of(t)
        grads = obuf[pl.ds(t * TILE, TILE)]
        for i in tiles:
            rows = pl.ds(i * TILE, TILE)
            keys = kbuf[rows]
            kp = jnp.concatenate([kpos[rows], kpos[rows]], axis=1)
            s = jnp.where((kp >= first2) & (kp <= qpos2), dot(keys, qt) * SCALE, FAR_BELOW)
            sc[t, rows] = s
            dp[t, rows] = dot(keys[:, :512], grads, NT)
            top = jnp.max(s, axis=0, keepdims=True)
            most[t] = jnp.maximum(most[t], top) if t in most else top

    def weights(t):
        total[t] = weighted[t] = jnp.zeros((1, TILE), F32)
        for i in range(4):
            rows = pl.ds(i * TILE, TILE)
            e = jnp.exp(sc[t, rows] - most[t])
            sc[t, rows] = e
            total[t] += jnp.sum(e, axis=0, keepdims=True)
            weighted[t] += jnp.sum(e * dp[t, rows], axis=0, keepdims=True)
        for n, value in enumerate((most[t], total[t], weighted[t])):
            for half in range(2):
                stat[0, pl.ds(n * 8 + absolute(2 * t + half), 1), :] = value[:, half * 128:(half + 1) * 128]

    def keys_in(offsets):
        for o in offsets:
            if o not in hubs:
                karrived(o)
                share(o)

    def other_keys_in(offsets):
        for o in offsets:
            i = index(o)
            remote(chunk(o), chunk(o, 1), kc_s.at[i], kc_r.at[i], me).wait_recv()

    close = [o for o in waits if index(o) < 8]
    distant = [o for o in waits if index(o) >= 8]
    keys_in(close)
    other_keys_in([0] + close)
    scores(0, (0, 2))
    keys_in(distant)
    arrived_o(6)
    arrived_q(2)
    for t, slot in ((1, 3), (3, 7)):
        arrived_q(slot)
        arrived_o(slot)
        scores(t, (0, 2))
    other_keys_in(distant)
    for t in (0, 1, 3):
        scores(t, (1, 3))
        weights(t)
    arrived_q(5)
    arrived_o(5)
    scores(2, range(4))
    weights(2)

    for j in (4, 5, 3, 7, 1, 2, 6):
        back = ((-(j // 2)) % NX) * 2 + j % 2
        send(stat.at[0], stat.at[back], st_s.at[j], st_r.at[back], at(dx=j // 2, dyl=j % 2))
    ktr[...] = kbuf[...].T
    for j in range(1, 8):
        remote(stat.at[0], stat.at[j], st_s.at[j], st_r.at[j], me).wait_recv()
    top = stat[0, 0:8]
    for j in range(1, 8):
        top = jnp.maximum(top, stat[j, 0:8])
    whole_total, whole_weighted = jnp.zeros((8, 128), F32), jnp.zeros((8, 128), F32)
    for j in range(8):
        factor = jnp.exp(stat[j, 0:8] - top)
        whole_total += stat[j, 8:16] * factor
        whole_weighted += stat[j, 16:24] * factor
    comb[0:8] = jnp.exp(stat[0, 0:8] - top) / whole_total
    comb[8:16] = whole_weighted / whole_total

    def grads_of(i):
        rows = pl.ds(i * TILE, TILE)
        for t in range(4):
            gain, centre = (
                jnp.concatenate([comb[pl.ds(n * 8 + absolute(2 * t + half), 1), :] for half in range(2)], axis=1) for n in range(2))
            p = sc[t, rows] * gain
            sg[rows, t * TILE:(t + 1) * TILE] = (p * (dp[t, rows] - centre) * SCALE).astype(BF16)
            pr[rows, t * TILE:(t + 1) * TILE] = p.astype(BF16)

    def dk_tile(i, out, out_rows):
        rows = pl.ds(i * TILE, TILE)
        value = dot(pr[rows], obuf[...])
        whole = jnp.zeros((TILE, 576), F32)
        for t in range(4):
            whole += dot(sg[rows, t * TILE:(t + 1) * TILE], queries_of(t), NT)
        out[out_rows, :512] = (whole[:, :512] + value).astype(out.dtype)
        out[out_rows, 512:] = whole[:, 512:].astype(out.dtype)

    def dk_other(half):
        rows = pl.ds(half * TILE, TILE)
        dk_tile(2 + half, ksend, rows)
        send(ksend.at[rows], krecv.at[rows], dc_s.at[half], dc_r.at[half], at(dc=1))

    def dk_own(half):
        dk_tile(half, dk, pl.ds(half * TILE, TILE))

    def other_core(half):
        rows = pl.ds(half * TILE, TILE)
        remote(ksend.at[rows], krecv.at[rows], dc_s.at[half], dc_r.at[half], me).wait_recv()

    def part(o):
        rows = pl.ds(index(o) * 32, 32)
        acc = dk[rows] + krecv[rows].astype(F32)
        for source in children(REDUCE, o):
            i = index(source)
            remote(rs_send.at[i], rs_recv.at[i], rs_s.at[i], rs_r.at[i], me).wait_recv()
            acc += rs_recv[i].astype(F32)
        return acc

    def first_half(ref, o):
        return ref.at[index(o), pl.ds(0, PIECE)]

    def rs_pass(o):
        i = index(o)
        rs_send[i] = part(o).astype(BF16)
        if REDUCE[o] != 0:
            send(rs_send.at[i], rs_recv.at[i], rs_s.at[i], rs_r.at[i], at(dz=o - REDUCE[o]))
            return
        cross(o)
        send(first_half(rs_send, o), first_half(rs_recv, o), rs_s.at[i], rs_r.at[i], at(dz=o))

    def cross(o):
        i = index(o)
        send(rs_send.at[i, pl.ds(PIECE, PIECE)], cross_recv.at[i], cr_s.at[i], cr_r.at[i], at(dyh=1, dz=o))

    def dq_pair(t):
        both = dot(ktr[...], sg[:, t * TILE:(t + 1) * TILE])
        for half in range(2):
            j = 2 * t + half
            value = both[:, half * 128:(half + 1) * 128]
            if j == 0:
                dq_own[...] = value
                continue
            dq_send[j] = value.astype(BF16)
            back = ((-(j // 2)) % NX) * 2 + j % 2
            send(dq_send.at[j], dq_recv.at[back], dq_s.at[j], dq_r.at[back], at(dx=j // 2, dyl=j % 2))

    leaves = sorted((o for o in REDUCE if not children(REDUCE, o)), key=lambda o: (-abs(o), -o))
    inner = sorted((o for o in REDUCE if children(REDUCE, o)), key=lambda o: (-abs(o), -o))
    early = [o for o in leaves if index(o) >= 8]
    for i in (3, 1, 2, 0):
        grads_of(i)
    dq_pair(2)
    dk_other(1)
    dk_own(1)
    dq_pair(1)
    other_core(1)
    for o in early:
        rs_pass(o)
    dq_pair(3)
    dk_other(0)
    dk_own(0)
    other_core(0)
    for o in leaves:
        if o not in early:
            rs_pass(o)
    rows = pl.ds(index(0) * 32 + PIECE, PIECE)
    rs_send[index(0), PIECE:] = (dk[rows] + krecv[rows].astype(F32)).astype(BF16)
    cross(0)
    for o in inner[:2]:
        rs_pass(o)
    dq_pair(0)
    for o in inner[2:]:
        rs_pass(o)
    dq = dq_own[...]
    for j in (1, 2, 3, 6, 7, 4, 5):
        remote(dq_send.at[j], dq_recv.at[j], dq_s.at[j], dq_r.at[j], me).wait_recv()
        dq += dq_recv[j].astype(F32)
    dq_out[...] = dq.astype(BF16)
    rows = pl.ds(index(0) * 32, PIECE)
    total = dk[rows] + krecv[rows].astype(F32)
    for o in children(REDUCE, 0):
        i = index(o)
        remote(first_half(rs_send, o), first_half(rs_recv, o), rs_s.at[i], rs_r.at[i], me).wait_recv()
        total += rs_recv[i, :PIECE].astype(F32)
    for o in [0] + children(REDUCE, 0):
        i = index(o)
        remote(rs_send.at[i, pl.ds(PIECE, PIECE)], cross_recv.at[i], cr_s.at[i], cr_r.at[i], me).wait_recv()
        total += cross_recv[i].astype(F32)
    dk_out[...] = total.astype(BF16)
    for copy in pending:
        copy.wait_send()


def local(latent, queries, grad_out, doc_lengths):
    vmem = pl.BlockSpec(memory_space=pltpu.VMEM)
    hbm = pl.BlockSpec(memory_space=pltpu.HBM)
    sem = pltpu.SemaphoreType.DMA
    arrays = latent.T, queries.reshape(128, 576).T, grad_out.reshape(128, 512), doc_lengths
    dq, dk = pl.pallas_call(
        kernel,
        out_shape=(jax.ShapeDtypeStruct((576, 128), BF16), jax.ShapeDtypeStruct((PIECE, 576), BF16)),
        in_specs=[hbm, hbm, hbm, pl.BlockSpec(memory_space=pltpu.SMEM)],
        out_specs=(vmem, vmem),
        scratch_shapes=[
            pltpu.VMEM((576, 128), BF16),
            pltpu.VMEM((128, 576), BF16),
            pltpu.VMEM((1024, 576), BF16),
            pltpu.VMEM((576, 1024), BF16),
            pltpu.VMEM((1024, 128), jnp.int32),
            pltpu.VMEM((8, 576, 128), BF16),
            pltpu.VMEM((1024, 512), BF16),
            pltpu.VMEM((4, 1024, TILE), F32),
            pltpu.VMEM((4, 1024, TILE), F32),
            pltpu.VMEM((1024, 1024), BF16),
            pltpu.VMEM((1024, 1024), BF16),
            pltpu.VMEM((8, 24, 128), F32),
            pltpu.VMEM((16, 128), F32),
            pltpu.VMEM((512, 576), F32),
            pltpu.VMEM((512, 576), BF16),
            pltpu.VMEM((512, 576), BF16),
            pltpu.VMEM((NZ, 32, 576), BF16),
            pltpu.VMEM((NZ, 32, 576), BF16),
            pltpu.VMEM((NZ, PIECE, 576), BF16),
            pltpu.VMEM((8, 576, 128), BF16),
            pltpu.VMEM((8, 576, 128), BF16),
            pltpu.VMEM((576, 128), F32),
            sem((7,)), sem((8,)), sem((7,)), sem((8,)),
            sem((NZ,)), sem((NZ,)), sem((NZ,)), sem((NZ,)), sem((NZ,)), sem((NZ,)),
            sem((8,)), sem((8,)), sem((2,)), sem((2,)),
            sem((NZ,)), sem((NZ,)), sem((NZ,)), sem((NZ,)), sem((8,)), sem((8,)), sem((3,)),
        ],
        compiler_params=pltpu.CompilerParams(collective_id=0, has_side_effects=True, vmem_limit_bytes=48 << 20),
        cost_estimate=pl.CostEstimate(flops=6_000_000_000, bytes_accessed=1_000_000, transcendentals=1_100_000),
        name="latent_attention_backward",
    )(*(pltpu.with_memory_space_constraint(array, pltpu.HBM) for array in arrays))
    return dq.T.reshape(128, 1, 576), dk


def solution(mesh):
    placed = (P("seq", None), P("seq", "head", None), P("seq", "head", None), P())
    return jax.shard_map(
        local,
        mesh=mesh,
        in_specs=placed,
        out_specs=(P("seq", "head", None), P(("seq", "head"), None)),
        check_vma=False,
    )
```

```python
import jax
import jax.numpy as jnp
from jax import lax
from jax.experimental import pallas as pl
from jax.experimental.pallas import tpu as pltpu
from jax.sharding import PartitionSpec as P

MESH = pl.DeviceIdType.MESH
F32, BF16 = jnp.float32, jnp.bfloat16
SCALE = 0.07216878364870322
FAR_BELOW = -1e30
NX, NZ = 4, 16
PIECE = 16
TILE = 256
NT = (((1,), (1,)), ((), ()))
NN = (((1,), (0,)), ((), ()))


def dot(a, b, dims=NN):
    return lax.dot_general(a, b, dims, preferred_element_type=F32)


def tree(step):
    above = {}
    for o in range(1, 9):
        above[o] = (o - 1) // step * step
    for o in range(1, 8):
        above[-o] = -((o - 1) // step * step)
    return above


GATHER, REDUCE = tree(3), tree(2)


def children(above, o):
    return sorted((k for k in above if above[k] == o), key=lambda k: (k not in above.values(), -abs(k), k))


def index(o):
    return (o + 3) % NZ


def kernel(
    lat_ref, q_ref, do_ref, len_ref, dq_out, dk_out,
    lat, krows, kbuf, ktr, kpos, qbuf, obuf, sc, dp, sg, pr,
    stat, comb, dk, ksend, krecv, rs_send, rs_recv, cross_recv,
    dq_send, dq_recv, dq_own,
    gq_s, gq_r, go_s, go_r, kz_s, kz_r, ka_s, ka_r, kc_s, kc_r, st_s, st_r, dc_s, dc_r, rs_s, rs_r, cr_s, cr_r, dq_s, dq_r, here_s,
):
    seq, head = lax.axis_index("seq"), lax.axis_index("head")
    yh, z, c = seq // (2 * NZ), (seq // 2) % NZ, seq % 2
    x, yl = head // 2, head % 2

    def at(dx=0, dyl=0, dz=0, dc=0, dyh=0):
        seq_to = ((yh + dyh) % 2) * (2 * NZ) + ((z + dz + NZ) % NZ) * 2 + (c + dc) % 2
        return seq_to, ((x + dx + NX) % NX) * 2 + (yl + dyl) % 2

    me = at()
    pending = []
    near = children(GATHER, 0)

    def remote(src, dst, ssem, rsem, to):
        return pltpu.make_async_remote_copy(src, dst, ssem, rsem, device_id=to, device_id_type=MESH)

    def send(*args):
        copy = remote(*args)
        copy.start()
        pending.append(copy)

    def sent(count):
        for copy in pending[:count]:
            copy.wait_send()
        del pending[:count]

    own = [
        pltpu.make_async_copy(lat_ref, lat, here_s.at[0]),
        pltpu.make_async_copy(q_ref, qbuf.at[0], here_s.at[1]),
        pltpu.make_async_copy(do_ref, obuf.at[pl.ds(0, 128)], here_s.at[2]),
    ]
    for copy in own:
        copy.start()
    peers = [at(dx=j // 2, dyl=j % 2) for j in range(1, 8)]
    peers += [at(dz=o) for o in near]
    peers += [at(dyh=1, dyl=1, dz=o) for o in [0] + near]
    peers += [at(dyh=1, dz=o) for o in [0] + near]
    peers += [at(dc=1)]
    barrier = pltpu.get_barrier_semaphore()
    for peer in peers:
        pl.semaphore_signal(barrier, inc=1, device_id=peer, device_id_type=MESH)
    own[0].wait()
    krows[...] = lat[...].T
    own[1].wait()
    own[2].wait()
    pl.semaphore_wait(barrier, len(peers))

    def grad_rows(slot):
        return obuf.at[pl.ds(slot * 128, 128)]

    def gather_q(n, src, slot, to):
        send(qbuf.at[src], qbuf.at[slot], gq_s.at[n], gq_r.at[slot], to)

    def gather_o(n, src, slot, to):
        send(grad_rows(src), grad_rows(slot), go_s.at[n], go_r.at[slot], to)

    def gather(n, src, slot, to):
        gather_q(n, src, slot, to)
        gather_o(n, src, slot, to)

    def arrived_q(slot):
        remote(qbuf.at[0], qbuf.at[slot], gq_s.at[0], gq_r.at[slot], me).wait_recv()

    def arrived_o(slot):
        remote(grad_rows(0), grad_rows(slot), go_s.at[0], go_r.at[slot], me).wait_recv()

    def chunk(o, core=0):
        return kbuf.at[pl.ds(core * 512 + index(o) * 32, 32)]

    def piece(o, plane):
        return kbuf.at[pl.ds(index(o) * 32 + plane * PIECE, PIECE)]

    own_piece = krows.at[pl.ds(pl.multiple_of(head * PIECE, PIECE), PIECE)]
    their_piece = krows.at[pl.ds(pl.multiple_of((x * 2 + (1 - yl)) * PIECE, PIECE), PIECE)]

    def first_spread(o):
        i = index(o)
        if o != 0:
            send(own_piece, piece(o, 0), kz_s.at[i], kz_r.at[i], at(dz=-o))
        send(their_piece, piece(o, 1), ka_s.at[i], ka_r.at[i], at(dyh=1, dyl=1, dz=-o))

    def share(o):
        i = index(o)
        send(chunk(o), chunk(o, 1), kc_s.at[i], kc_r.at[i], at(dc=1))

    def spread(o):
        for to in children(GATHER, o):
            n = index(to)
            send(chunk(o), chunk(to), kz_s.at[n], kz_r.at[n], at(dz=o - to))
        share(o)

    def karrived(o):
        i = index(o)
        if o in near:
            remote(own_piece, piece(o, 0), kz_s.at[i], kz_r.at[i], me).wait_recv()
        elif o != 0:
            remote(chunk(o), chunk(o), kz_s.at[i], kz_r.at[i], me).wait_recv()
        if o in near or o == 0:
            remote(their_piece, piece(o, 1), ka_s.at[i], ka_r.at[i], me).wait_recv()

    for o in near[:2]:
        first_spread(o)
    gather(0, 0, 6, at(dx=1))
    gather(1, 0, 2, at(dx=-1))
    gather(2, 0, 1, at(dyl=1))
    for o in [0] + near[2:]:
        first_spread(o)
    kbuf[pl.ds(index(0) * 32, PIECE)] = krows[pl.ds(pl.multiple_of(head * PIECE, PIECE), PIECE)]

    row = lax.broadcasted_iota(jnp.int32, kpos.shape, 0)
    r_c, r_z, r_y = row // 512, (row // 32) % NZ, (row // PIECE) % 2
    k_c, k_z, k_y = (c + r_c) % 2, (z + r_z + NZ - 3) % NZ, (yh + r_y) % 2
    kpos[...] = (k_y * (2 * NZ) + k_z * 2 + k_c) * 128 + head * PIECE + row % PIECE
    qpos = seq * 128 + lax.broadcasted_iota(jnp.int32, (1, 128), 1)
    first = jnp.zeros((1, 128), jnp.int32)
    start = jnp.int32(0)
    for d in range(8):
        first = jnp.where(qpos >= start, start, first)
        start = start + len_ref[d]
    qpos2 = jnp.concatenate([qpos, qpos], axis=1)
    first2 = jnp.concatenate([first, first], axis=1)
    waits = sorted(GATHER, key=lambda o: (abs(o), -o))
    hubs = [o for o in waits if children(GATHER, o)]
    for o in hubs[:2]:
        karrived(o)
        spread(o)
    arrived_q(6)
    gather_q(3, 6, 4, at(dx=1))
    arrived_o(2)
    gather_o(3, 2, 4, at(dx=-1))
    karrived(0)
    share(0)
    arrived_q(1)
    gather_q(4, 1, 7, at(dx=1))
    gather_q(5, 1, 3, at(dx=-1))
    arrived_o(1)
    gather_o(4, 1, 7, at(dx=1))
    gather_o(5, 1, 3, at(dx=-1))
    for o in hubs[2:]:
        karrived(o)
        spread(o)
    arrived_q(4)
    gather_q(6, 4, 5, at(dyl=1))
    arrived_o(4)
    gather_o(6, 4, 5, at(dyl=1))
    most, total, weighted = {}, {}, {}

    def absolute(slot):
        return ((x + slot // 2) % NX) * 2 + (yl + slot % 2) % 2

    def queries_of(t):
        return jnp.concatenate([qbuf[2 * t], qbuf[2 * t + 1]], axis=1)

    def scores(t, tiles):
        qt = queries_of(t)
        grads = obuf[pl.ds(t * TILE, TILE)]
        for i in tiles:
            rows = pl.ds(i * TILE, TILE)
            keys = kbuf[rows]
            kp = jnp.concatenate([kpos[rows], kpos[rows]], axis=1)
            s = jnp.where((kp >= first2) & (kp <= qpos2), dot(keys, qt) * SCALE, FAR_BELOW)
            sc[t, rows] = s
            dp[t, rows] = dot(keys[:, :512], grads, NT)
            top = jnp.max(s, axis=0, keepdims=True)
            most[t] = jnp.maximum(most[t], top) if t in most else top

    def weights(t):
        total[t] = weighted[t] = jnp.zeros((1, TILE), F32)
        for i in range(4):
            rows = pl.ds(i * TILE, TILE)
            e = jnp.exp(sc[t, rows] - most[t])
            sc[t, rows] = e
            total[t] += jnp.sum(e, axis=0, keepdims=True)
            weighted[t] += jnp.sum(e * dp[t, rows], axis=0, keepdims=True)
        for n, value in enumerate((most[t], total[t], weighted[t])):
            for half in range(2):
                stat[0, pl.ds(n * 8 + absolute(2 * t + half), 1), :] = value[:, half * 128:(half + 1) * 128]

    def keys_in(offsets):
        for o in offsets:
            if o not in hubs:
                karrived(o)
                share(o)

    def other_keys_in(offsets):
        for o in offsets:
            i = index(o)
            remote(chunk(o), chunk(o, 1), kc_s.at[i], kc_r.at[i], me).wait_recv()

    close = [o for o in waits if index(o) < 8]
    distant = [o for o in waits if index(o) >= 8]
    keys_in(close)
    other_keys_in([0] + close)
    scores(0, (0, 2))
    keys_in(distant)
    arrived_o(6)
    arrived_q(2)
    for t, slot in ((1, 3), (3, 7)):
        arrived_q(slot)
        arrived_o(slot)
        scores(t, (0, 2))
    other_keys_in(distant)
    for t in (0, 1, 3):
        scores(t, (1, 3))
        weights(t)
    arrived_q(5)
    arrived_o(5)
    scores(2, range(4))
    weights(2)

    for j in (4, 5, 3, 7, 1, 2, 6):
        back = ((-(j // 2)) % NX) * 2 + j % 2
        send(stat.at[0], stat.at[back], st_s.at[j], st_r.at[back], at(dx=j // 2, dyl=j % 2))
    sent(len(pending) - 7)
    ktr[...] = kbuf[...].T
    for j in range(1, 8):
        remote(stat.at[0], stat.at[j], st_s.at[j], st_r.at[j], me).wait_recv()
    top = stat[0, 0:8]
    for j in range(1, 8):
        top = jnp.maximum(top, stat[j, 0:8])
    whole_total, whole_weighted = jnp.zeros((8, 128), F32), jnp.zeros((8, 128), F32)
    for j in range(8):
        factor = jnp.exp(stat[j, 0:8] - top)
        whole_total += stat[j, 8:16] * factor
        whole_weighted += stat[j, 16:24] * factor
    comb[0:8] = jnp.exp(stat[0, 0:8] - top) / whole_total
    comb[8:16] = whole_weighted / whole_total

    def grads_of(i):
        rows = pl.ds(i * TILE, TILE)
        for t in range(4):
            gain, centre = (
                jnp.concatenate([comb[pl.ds(n * 8 + absolute(2 * t + half), 1), :] for half in range(2)], axis=1) for n in range(2))
            p = sc[t, rows] * gain
            sg[rows, t * TILE:(t + 1) * TILE] = (p * (dp[t, rows] - centre) * SCALE).astype(BF16)
            pr[rows, t * TILE:(t + 1) * TILE] = p.astype(BF16)

    def dk_tile(i, out, out_rows):
        rows = pl.ds(i * TILE, TILE)
        value = dot(pr[rows], obuf[...])
        whole = jnp.zeros((TILE, 576), F32)
        for t in range(4):
            whole += dot(sg[rows, t * TILE:(t + 1) * TILE], queries_of(t), NT)
        out[out_rows, :512] = (whole[:, :512] + value).astype(out.dtype)
        out[out_rows, 512:] = whole[:, 512:].astype(out.dtype)

    def dk_other(half):
        rows = pl.ds(half * TILE, TILE)
        dk_tile(2 + half, ksend, rows)
        send(ksend.at[rows], krecv.at[rows], dc_s.at[half], dc_r.at[half], at(dc=1))

    def dk_own(half):
        dk_tile(half, dk, pl.ds(half * TILE, TILE))

    def other_core(half):
        rows = pl.ds(half * TILE, TILE)
        remote(ksend.at[rows], krecv.at[rows], dc_s.at[half], dc_r.at[half], me).wait_recv()

    def part(o):
        rows = pl.ds(index(o) * 32, 32)
        acc = dk[rows] + krecv[rows].astype(F32)
        for source in children(REDUCE, o):
            i = index(source)
            remote(rs_send.at[i], rs_recv.at[i], rs_s.at[i], rs_r.at[i], me).wait_recv()
            acc += rs_recv[i].astype(F32)
        return acc

    def first_half(ref, o):
        return ref.at[index(o), pl.ds(0, PIECE)]

    def rs_pass(o):
        i = index(o)
        rs_send[i] = part(o).astype(BF16)
        if REDUCE[o] != 0:
            send(rs_send.at[i], rs_recv.at[i], rs_s.at[i], rs_r.at[i], at(dz=o - REDUCE[o]))
            return
        cross(o)
        send(first_half(rs_send, o), first_half(rs_recv, o), rs_s.at[i], rs_r.at[i], at(dz=o))

    def cross(o):
        i = index(o)
        send(rs_send.at[i, pl.ds(PIECE, PIECE)], cross_recv.at[i], cr_s.at[i], cr_r.at[i], at(dyh=1, dz=o))

    def dq_pair(t):
        both = dot(ktr[...], sg[:, t * TILE:(t + 1) * TILE])
        for half in range(2):
            j = 2 * t + half
            value = both[:, half * 128:(half + 1) * 128]
            if j == 0:
                dq_own[...] = value
                continue
            dq_send[j] = value.astype(BF16)
            back = ((-(j // 2)) % NX) * 2 + j % 2
            send(dq_send.at[j], dq_recv.at[back], dq_s.at[j], dq_r.at[back], at(dx=j // 2, dyl=j % 2))

    leaves = sorted((o for o in REDUCE if not children(REDUCE, o)), key=lambda o: (-abs(o), -o))
    inner = sorted((o for o in REDUCE if children(REDUCE, o)), key=lambda o: (-abs(o), -o))
    early = [o for o in leaves if index(o) >= 8]
    for i in (3, 1, 2, 0):
        grads_of(i)
    dq_pair(2)
    dk_other(1)
    dk_own(1)
    dq_pair(1)
    other_core(1)
    for o in early:
        rs_pass(o)
    dq_pair(3)
    dk_other(0)
    dk_own(0)
    other_core(0)
    for o in leaves:
        if o not in early:
            rs_pass(o)
    rows = pl.ds(index(0) * 32 + PIECE, PIECE)
    rs_send[index(0), PIECE:] = (dk[rows] + krecv[rows].astype(F32)).astype(BF16)
    cross(0)
    for o in inner[:2]:
        rs_pass(o)
    dq_pair(0)
    for o in inner[2:]:
        rs_pass(o)
    sent(7 + 2)
    dq = dq_own[...]
    for j in (1, 2, 3, 6, 7, 4, 5):
        remote(dq_send.at[j], dq_recv.at[j], dq_s.at[j], dq_r.at[j], me).wait_recv()
        dq += dq_recv[j].astype(F32)
    dq_out[...] = dq.astype(BF16)
    rows = pl.ds(index(0) * 32, PIECE)
    total = dk[rows] + krecv[rows].astype(F32)
    for o in children(REDUCE, 0):
        i = index(o)
        remote(first_half(rs_send, o), first_half(rs_recv, o), rs_s.at[i], rs_r.at[i], me).wait_recv()
        total += rs_recv[i, :PIECE].astype(F32)
    for o in [0] + children(REDUCE, 0):
        i = index(o)
        remote(rs_send.at[i, pl.ds(PIECE, PIECE)], cross_recv.at[i], cr_s.at[i], cr_r.at[i], me).wait_recv()
        total += cross_recv[i].astype(F32)
    dk_out[...] = total.astype(BF16)
    sent(len(pending))


def local(latent, queries, grad_out, doc_lengths):
    vmem = pl.BlockSpec(memory_space=pltpu.VMEM)
    hbm = pl.BlockSpec(memory_space=pltpu.HBM)
    sem = pltpu.SemaphoreType.DMA
    arrays = latent.T, queries.reshape(128, 576).T, grad_out.reshape(128, 512), doc_lengths
    dq, dk = pl.pallas_call(
        kernel,
        out_shape=(jax.ShapeDtypeStruct((576, 128), BF16), jax.ShapeDtypeStruct((PIECE, 576), BF16)),
        in_specs=[hbm, hbm, hbm, pl.BlockSpec(memory_space=pltpu.SMEM)],
        out_specs=(vmem, vmem),
        scratch_shapes=[
            pltpu.VMEM((576, 128), BF16),
            pltpu.VMEM((128, 576), BF16),
            pltpu.VMEM((1024, 576), BF16),
            pltpu.VMEM((576, 1024), BF16),
            pltpu.VMEM((1024, 128), jnp.int32),
            pltpu.VMEM((8, 576, 128), BF16),
            pltpu.VMEM((1024, 512), BF16),
            pltpu.VMEM((4, 1024, TILE), F32),
            pltpu.VMEM((4, 1024, TILE), F32),
            pltpu.VMEM((1024, 1024), BF16),
            pltpu.VMEM((1024, 1024), BF16),
            pltpu.VMEM((8, 24, 128), F32),
            pltpu.VMEM((16, 128), F32),
            pltpu.VMEM((512, 576), F32),
            pltpu.VMEM((512, 576), BF16),
            pltpu.VMEM((512, 576), BF16),
            pltpu.VMEM((NZ, 32, 576), BF16),
            pltpu.VMEM((NZ, 32, 576), BF16),
            pltpu.VMEM((NZ, PIECE, 576), BF16),
            pltpu.VMEM((8, 576, 128), BF16),
            pltpu.VMEM((8, 576, 128), BF16),
            pltpu.VMEM((576, 128), F32),
            sem((7,)), sem((8,)), sem((7,)), sem((8,)),
            sem((NZ,)), sem((NZ,)), sem((NZ,)), sem((NZ,)), sem((NZ,)), sem((NZ,)),
            sem((8,)), sem((8,)), sem((2,)), sem((2,)),
            sem((NZ,)), sem((NZ,)), sem((NZ,)), sem((NZ,)), sem((8,)), sem((8,)), sem((3,)),
        ],
        compiler_params=pltpu.CompilerParams(collective_id=0, has_side_effects=True, vmem_limit_bytes=48 << 20),
        cost_estimate=pl.CostEstimate(flops=6_000_000_000, bytes_accessed=1_000_000, transcendentals=1_100_000),
        name="latent_attention_backward",
    )(*(pltpu.with_memory_space_constraint(array, pltpu.HBM) for array in arrays))
    return dq.T.reshape(128, 1, 576), dk


def solution(mesh):
    placed = (P("seq", None), P("seq", "head", None), P("seq", "head", None), P())
    return jax.shard_map(
        local,
        mesh=mesh,
        in_specs=placed,
        out_specs=(P("seq", "head", None), P(("seq", "head"), None)),
        check_vma=False,
    )
```
